512 devices in a mesh: ctx: 64 (over x_lo, z, core), tp: 8 (over x_hi, y).
Axes of the slice: x: 4 (x_hi: 2, x_lo: 2; x = x_hi * 2 + x_lo), y: 4, z: 16, core: 2. Of those that a mesh axis runs over, the one named last changes fastest.
Arguments:
- query: bfloat16 [8192, 4096], P('ctx', 'tp'), as said below
- key_proj: bfloat16 [8192, 4096], P('ctx', 'tp'), may hold values from -6 to 6
- value_proj: bfloat16 [8192, 4096], P('ctx', 'tp'), may hold values from -6 to 6
- filter_taps: bfloat16 [8192, 4096], P('ctx', 'tp'), may hold values from -6 to 6
- grad_out: bfloat16 [8192, 4096], P('ctx', 'tp'), may hold values from -6 to 6
Outputs:
- mixer_out: bfloat16 [8192, 4096], P('ctx', 'tp')
- dquery: bfloat16 [8192, 4096], P('ctx', 'tp')
- dkey: bfloat16 [8192, 4096], P('ctx', 'tp')
- dvalue: bfloat16 [8192, 4096], P('ctx', 'tp')
- dtaps: bfloat16 [8192, 4096], P('ctx', 'tp')
The draws below stay inside these ranges and needn't reach their ends.
Inputs may be any that keep to these rules, and one draw needn't show every extreme that they name: Entries of query are real values of either sign.
All inputs are finite; a program needn't handle non-finite values.
Results may differ from the reference program's by a relative error of at most 0.0085.
Values may be sent and summed in bfloat16 or wider, within the bound.
A program may use at most 64 MiB of HBM per device.

```python
import math
import jax
import jax.numpy as jnp
from jax import lax

W = 4096
L = 8192


def draw_query(key, part):
    first_key, second_key = jax.random.split(key, 2)
    channel_pos = jnp.arange(W, dtype=jnp.float32) / W
    spread = jnp.exp(jax.random.uniform(second_key, (W,), jnp.float32, 0.0, math.log(10.0)))
    column_scale = spread * 3.0 ** channel_pos
    base = jnp.clip(jax.random.normal(first_key, (L, W), jnp.float32), -6.0, 6.0)
    return (0.3 * base * column_scale[None, :]).astype(jnp.bfloat16)


def steps_of(stream_key, shape, pieces, low, top_value):
    loudness, own = 1.0, jax.random.fold_in(stream_key, 6)
    for axis_at, blocks in pieces:
        heights = jnp.exp(jax.random.uniform(jax.random.fold_in(own, axis_at), (blocks,), jnp.float32, low / len(pieces), top_value / len(pieces)))
        loudness = loudness * jnp.repeat(heights, shape[axis_at] // blocks).reshape([-1 if axis == axis_at else 1 for axis in range(len(shape))])
    return loudness


def normal_values(key, extent, scale, most, cuts=(), held_as=jnp.bfloat16):
    array = jax.random.normal(key, extent, jnp.float32) * scale
    if len(cuts) > 0:
        array = steps_of(key, extent, cuts, -0.22, 0.18) * array
    return jnp.clip(array, min=-most, max=most).astype(held_as)


def setup_inputs(seed: int = 0) -> dict:
    streams_of = jax.random.split(jax.random.key(seed), 6)
    query = draw_query(jax.random.fold_in(streams_of[5], 71), 0)
    key_proj = normal_values(streams_of[1], (L, W), 1.0, 6.0, ((0, 64), (1, 8)))
    value_proj = normal_values(streams_of[2], (L, W), 1.0, 6.0, ((0, 64), (1, 8)))
    filter_taps = normal_values(streams_of[3], (L, W), 1.0, 6.0, ((0, 64), (1, 8)))
    grad_out = normal_values(streams_of[4], (L, W), 1.0, 6.0, ((0, 64), (1, 8)))
    return dict(query=query, key_proj=key_proj, value_proj=value_proj, filter_taps=filter_taps, grad_out=grad_out)


def column_groups(matrix):
    length, width = matrix.shape
    group_size = min(width, 512)
    return matrix.reshape(length, width // group_size, group_size).transpose(1, 0, 2)

def joined(groups):
    group_count, length, group_size = groups.shape
    return groups.transpose(1, 0, 2).reshape(length, group_count * group_size)

def causal_filter(operands):
    taps, signal = operands
    length = taps.shape[0]
    spectrum = jnp.fft.rfft(taps, n=2 * length, axis=0) * jnp.fft.rfft(signal, n=2 * length, axis=0)
    return jnp.fft.irfft(spectrum, n=2 * length, axis=0)[:length]

def correlation(operands):
    later, earlier = operands
    length = later.shape[0]
    spectrum = jnp.fft.rfft(later, n=2 * length, axis=0) * jnp.conj(jnp.fft.rfft(earlier, n=2 * length, axis=0))
    return jnp.fft.irfft(spectrum, n=2 * length, axis=0)[:length]

def reference(query, key_proj, value_proj, filter_taps, grad_out):
    filter_scale = 1.0 / math.sqrt(L)
    key_float = key_proj.astype(jnp.float32)
    value_float = value_proj.astype(jnp.float32)
    mixed_rows = lax.optimization_barrier((key_float * value_float).astype(jnp.bfloat16))
    mixed_float = mixed_rows.astype(jnp.float32)
    taps_float = filter_taps.astype(jnp.float32)
    conv_full = filter_scale * joined(lax.map(causal_filter, (column_groups(taps_float), column_groups(mixed_float))))
    conv_rows = lax.optimization_barrier(conv_full.astype(jnp.bfloat16))
    conv_float = conv_rows.astype(jnp.float32)
    query_float = query.astype(jnp.float32)
    gated = query_float * conv_float
    inverse_rms = lax.rsqrt(lax.optimization_barrier(jnp.mean(gated * gated, axis=1)) + 1e-05)
    mixer_out = (gated * inverse_rms[:, None]).astype(jnp.bfloat16)
    upstream = grad_out.astype(jnp.float32)
    dots = lax.optimization_barrier(jnp.mean(upstream * gated, axis=1))
    dgated = inverse_rms[:, None] * upstream - (inverse_rms ** 3 * dots)[:, None] * gated
    dquery = (dgated * conv_float).astype(jnp.bfloat16)
    gconv = lax.optimization_barrier((dgated * query_float).astype(jnp.bfloat16))
    gconv_float = gconv.astype(jnp.float32)
    dmixed_full = filter_scale * joined(lax.map(correlation, (column_groups(gconv_float), column_groups(taps_float))))
    dmixed = lax.optimization_barrier(dmixed_full.astype(jnp.bfloat16))
    dtaps_full = filter_scale * joined(lax.map(correlation, (column_groups(gconv_float), column_groups(mixed_float))))
    dtaps = dtaps_full.astype(jnp.bfloat16)
    dmixed_float = dmixed.astype(jnp.float32)
    dkey = (dmixed_float * value_float).astype(jnp.bfloat16)
    dvalue = (dmixed_float * key_float).astype(jnp.bfloat16)
    return (mixer_out, dquery, dkey, dvalue, dtaps)
```

```python
import functools
import math

import jax
import jax.numpy as jnp
import ml_dtypes
import numpy as np
from jax import lax
from jax.experimental import pallas as pl
from jax.experimental.pallas import tpu as pltpu
from jax.sharding import PartitionSpec as P

MESH = pl.DeviceIdType.MESH
F32 = jnp.float32
BF16 = jnp.bfloat16
EPS = 1e-05


def halves(table):
    high = table.astype(ml_dtypes.bfloat16)
    low = (table - high.astype(np.float64)).astype(ml_dtypes.bfloat16)
    return high, low


def tables(blocks, lanes):
    total = blocks * lanes
    i = np.arange(blocks, dtype=np.float64)
    j = np.arange(lanes, dtype=np.float64)
    outer = 2 * np.pi * np.outer(i + 0.25, i) / blocks
    first = np.concatenate([np.cos(outer), -np.sin(outer)], axis=0)
    first_high, first_low = halves(first)
    first_table = np.concatenate([first_high, first_low], axis=1)
    last_high, last_low = halves(np.ascontiguousarray(first.T))
    last_table = np.concatenate([last_high, last_high, last_low], axis=1)
    turn = 2 * np.pi * np.outer(i + 0.25, j) / total
    inner = 2 * np.pi * (np.outer(j, j) % lanes) / lanes
    cos, sin = np.cos(inner), np.sin(inner)
    ahead = np.block([[cos, -sin], [sin, cos]])
    back = np.block([[cos, sin], [-sin, cos]])
    inner_tables = []
    for table in (ahead, back):
        high, low = halves(table)
        inner_tables.append(np.concatenate([high, high, low], axis=0))
    return (
        first_table,
        last_table,
        inner_tables[0],
        inner_tables[1],
        np.cos(turn).astype(np.float32),
        np.sin(turn).astype(np.float32),
    )


def split(values):
    high = values.astype(BF16)
    return high, (values - high.astype(F32)).astype(BF16)


def dot(left, right):
    return jnp.dot(left, right, preferred_element_type=F32)


def kernel(
    n, m, width, scale,
    query_ref, key_ref, value_ref, taps_ref, grad_ref,
    first_ref, last_ref, ahead_ref, back_ref, cos_ref, sin_ref,
    mixer_ref, dquery_ref, dkey_ref, dvalue_ref, dtaps_ref,
    send1, recv1, send2, recv2, send3, recv3, send4, recv4,
    stat_out, stat_in, shuffle, query_t, grad_t, conv_t, taps_spec, mixed_spec,
    send_sem, recv_sem,
):
    me = lax.axis_index("ctx")
    mine = lax.axis_index("tp")
    rows, cols = query_ref.shape
    group = cols // n
    chips = n // 4

    barrier = pltpu.get_barrier_semaphore()

    def greet_ctx(step, carry):
        peer = lax.rem(me + step, n)
        pl.semaphore_signal(barrier, inc=1, device_id=(peer, mine), device_id_type=MESH)
        return carry

    def greet_tp(step, carry):
        peer = lax.rem(mine + step, m)
        pl.semaphore_signal(barrier, inc=1, device_id=(me, peer), device_id_type=MESH)
        return carry

    lax.fori_loop(1, n, greet_ctx, 0)
    lax.fori_loop(1, m, greet_tp, 0)

    def exchange(phase, source, target):
        side = me // (2 * chips)
        place = lax.rem(me // 2, chips)
        core = lax.rem(me, 2)

        def start(step, carry):
            quarter = lax.rem(step, 4)
            turn = step // 4
            half = lax.rem(turn, 2)
            far = jnp.where(half == 0, chips // 2 + turn // 2, chips // 2 - (turn + 1) // 2)
            flip = quarter // 2
            swap = lax.rem(quarter, 2)
            peer = (
                lax.rem(side + flip, 2) * (2 * chips)
                + lax.rem(place + far, chips) * 2
                + lax.rem(core + swap, 2)
            )
            pltpu.make_async_remote_copy(
                src_ref=source.at[peer],
                dst_ref=target.at[me],
                send_sem=send_sem.at[phase],
                recv_sem=recv_sem.at[phase],
                device_id=(peer, mine),
                device_id_type=MESH,
            ).start()
            return carry

        lax.fori_loop(0, n - 4, start, 0)
        lax.fori_loop(n - 3, n, start, 0)
        target[me] = source[me]

    def arrived(phase, source, target):
        pltpu.make_async_copy(
            source.at[pl.ds(0, n - 1)], target.at[pl.ds(0, n - 1)], recv_sem.at[phase]
        ).wait()

    def sent(phase, source, target):
        pltpu.make_async_copy(
            source.at[pl.ds(0, n - 1)], target.at[pl.ds(0, n - 1)], send_sem.at[phase]
        ).wait()

    def stage_first(blocks):
        shuffle[...] = blocks.astype(F32).reshape(n * group, rows)
        columns = jnp.concatenate(
            [shuffle[pl.ds(c, n, stride=group), :].astype(BF16) for c in range(group)], axis=1
        )
        outer = dot(first_ref[...], jnp.concatenate([columns, columns], axis=0))
        cos, sin = cos_ref[...], sin_ref[...]
        turned = []
        for c in range(group):
            real = outer[:n, c * rows : (c + 1) * rows]
            imag = outer[n:, c * rows : (c + 1) * rows]
            turned.append(
                jnp.concatenate([real * cos + imag * sin, imag * cos - real * sin], axis=1)
            )
        high, low = split(jnp.concatenate(turned, axis=0))
        return dot(jnp.concatenate([high, low, high], axis=1), ahead_ref[...])

    def stage_last(real, imag):
        high, low = split(jnp.concatenate([real, imag], axis=1))
        inner = dot(jnp.concatenate([high, low, high], axis=1), back_ref[...])
        cos, sin = cos_ref[...], sin_ref[...]
        turned = []
        for c in range(group):
            real = inner[c * n : (c + 1) * n, :rows]
            imag = inner[c * n : (c + 1) * n, rows:]
            turned.append(
                jnp.concatenate([real * cos - imag * sin, real * sin + imag * cos], axis=0)
            )
        high, low = split(jnp.concatenate(turned, axis=1))
        outer = dot(last_ref[...], jnp.concatenate([high, low, high], axis=0))
        for c in range(group):
            shuffle[pl.ds(c, n, stride=group), :] = outer[:, c * rows : (c + 1) * rows] * scale
        return shuffle[...].reshape(n, group, rows)

    mixed = (key_ref[...].astype(F32) * value_ref[...].astype(F32)).astype(BF16).astype(F32)
    send1[:, :group, :] = mixed.T.reshape(n, group, rows).astype(BF16)
    send1[:, group:, :] = taps_ref[...].astype(F32).T.reshape(n, group, rows).astype(BF16)
    pl.semaphore_wait(barrier, n + m - 2)
    exchange(0, send1, recv1)
    query_t[...] = query_ref[...].astype(F32).T
    grad_t[...] = grad_ref[...].astype(F32).T
    stat_out[...] = jnp.zeros_like(stat_out)
    arrived(0, send1, recv1)

    mixed_spec[...] = stage_first(recv1[:, :group, :])
    taps_spec[...] = stage_first(recv1[:, group:, :])
    mixed_real, mixed_imag = mixed_spec[:, :rows], mixed_spec[:, rows:]
    taps_real, taps_imag = taps_spec[:, :rows], taps_spec[:, rows:]
    send2[...] = stage_last(
        mixed_real * taps_real - mixed_imag * taps_imag,
        mixed_real * taps_imag + mixed_imag * taps_real,
    ).astype(BF16)
    exchange(1, send2, recv2)
    arrived(1, send2, recv2)

    conv_t[...] = recv2[...].astype(F32).reshape(cols, rows)
    gated = query_t[...] * conv_t[...]
    stat_out[0:1, :] = jnp.sum(gated * gated, axis=0, keepdims=True)
    stat_out[1:2, :] = jnp.sum(grad_t[...] * gated, axis=0, keepdims=True)

    def send_stats(step, carry):
        peer = lax.rem(mine + step, m)
        pltpu.make_async_remote_copy(
            src_ref=stat_out,
            dst_ref=stat_in.at[mine],
            send_sem=send_sem.at[4],
            recv_sem=recv_sem.at[4],
            device_id=(me, peer),
            device_id_type=MESH,
        ).start()
        return carry

    lax.fori_loop(1, m, send_stats, 0)
    stat_in[mine] = stat_out[...]
    pltpu.make_async_copy(
        stat_in.at[pl.ds(0, m - 1)], stat_in.at[pl.ds(0, m - 1)], recv_sem.at[4]
    ).wait()
    totals = jnp.sum(stat_in[...], axis=0)
    inverse_rms = lax.rsqrt(totals[0:1, :] / width + EPS)
    dots = totals[1:2, :] / width
    weight = inverse_rms * inverse_rms * inverse_rms * dots

    gated = query_t[...] * conv_t[...]
    dgated = inverse_rms * grad_t[...] - weight * gated
    send3[...] = (dgated * query_t[...]).astype(BF16).reshape(n, group, rows)
    exchange(2, send3, recv3)
    mixer_ref[...] = (gated * inverse_rms).T.astype(BF16)
    dquery_ref[...] = (dgated * conv_t[...]).T.astype(BF16)
    arrived(2, send3, recv3)

    grads = stage_first(recv3[...])
    grads_real, grads_imag = grads[:, :rows], grads[:, rows:]
    taps_real, taps_imag = taps_spec[:, :rows], taps_spec[:, rows:]
    send4[:, :group, :] = stage_last(
        grads_real * taps_real + grads_imag * taps_imag,
        grads_imag * taps_real - grads_real * taps_imag,
    ).astype(BF16)
    mixed_real, mixed_imag = mixed_spec[:, :rows], mixed_spec[:, rows:]
    send4[:, group:, :] = stage_last(
        grads_real * mixed_real + grads_imag * mixed_imag,
        grads_imag * mixed_real - grads_real * mixed_imag,
    ).astype(BF16)
    exchange(3, send4, recv4)
    arrived(3, send4, recv4)

    dmixed = recv4[:, :group, :].astype(F32).reshape(cols, rows).T
    dkey_ref[...] = (dmixed * value_ref[...].astype(F32)).astype(BF16)
    dvalue_ref[...] = (dmixed * key_ref[...].astype(F32)).astype(BF16)
    dtaps_ref[...] = recv4[:, group:, :].astype(F32).reshape(cols, rows).T.astype(BF16)

    sent(0, send1, recv1)
    sent(1, send2, recv2)
    sent(2, send3, recv3)
    sent(3, send4, recv4)
    pltpu.make_async_copy(
        stat_in.at[pl.ds(0, m - 1)], stat_in.at[pl.ds(0, m - 1)], send_sem.at[4]
    ).wait()


def per_device(n, m, query, key_proj, value_proj, filter_taps, grad_out):
    rows, cols = query.shape
    group = cols // n
    length = rows * n
    consts = [jnp.asarray(table) for table in tables(n, rows)]
    vmem = pl.BlockSpec(memory_space=pltpu.VMEM)
    one = pltpu.VMEM((n, group, rows), BF16)
    two = pltpu.VMEM((n, 2 * group, rows), BF16)
    wide = pltpu.VMEM((cols, rows), F32)
    return pl.pallas_call(
        functools.partial(kernel, n, m, cols * m, 1.0 / (math.sqrt(length) * length)),
        out_shape=[jax.ShapeDtypeStruct((rows, cols), BF16)] * 5,
        in_specs=[vmem] * 11,
        out_specs=[vmem] * 5,
        scratch_shapes=[
            two, two, one, one, one, one, two, two,
            pltpu.VMEM((8, rows), F32),
            pltpu.VMEM((m, 8, rows), F32),
            pltpu.VMEM((n * group, rows), F32),
            wide, wide, wide,
            pltpu.VMEM((n * group, 2 * rows), F32),
            pltpu.VMEM((n * group, 2 * rows), F32),
            pltpu.SemaphoreType.DMA((5,)),
            pltpu.SemaphoreType.DMA((5,)),
        ],
        compiler_params=pltpu.CompilerParams(
            collective_id=0, has_side_effects=True, vmem_limit_bytes=48 * 1024 * 1024
        ),
    )(query, key_proj, value_proj, filter_taps, grad_out, *consts)


def solution(mesh):
    spec = P("ctx", "tp")
    return jax.shard_map(
        functools.partial(per_device, mesh.shape["ctx"], mesh.shape["tp"]),
        mesh=mesh,
        in_specs=(spec,) * 5,
        out_specs=(spec,) * 5,
        check_vma=False,
    )
```

```python
import functools
import math

import jax
import jax.numpy as jnp
import ml_dtypes
import numpy as np
from jax import lax
from jax.experimental import pallas as pl
from jax.experimental.pallas import tpu as pltpu
from jax.sharding import PartitionSpec as P

MESH = pl.DeviceIdType.MESH
F32 = jnp.float32
BF16 = jnp.bfloat16
EPS = 1e-05
VMEM_BYTES = 63 * 1024 * 1024


def halves(table):
    high = table.astype(ml_dtypes.bfloat16)
    low = (table - high.astype(np.float64)).astype(ml_dtypes.bfloat16)
    return high, low


def tables(blocks, lanes):
    total = blocks * lanes
    i = np.arange(blocks, dtype=np.float64)
    j = np.arange(lanes, dtype=np.float64)
    outer = 2 * np.pi * np.outer(i + 0.25, i) / blocks
    first = np.concatenate([np.cos(outer), -np.sin(outer)], axis=0)
    first_high, first_low = halves(first)
    first_table = np.concatenate([first_high, first_low], axis=1)
    last_high, last_low = halves(np.ascontiguousarray(first.T))
    last_table = np.concatenate([last_high, last_high, last_low], axis=1)
    turn = 2 * np.pi * np.outer(i + 0.25, j) / total
    inner = 2 * np.pi * (np.outer(j, j) % lanes) / lanes
    cos, sin = np.cos(inner), np.sin(inner)
    ahead = np.block([[cos, -sin], [sin, cos]])
    back = np.block([[cos, sin], [-sin, cos]])
    inner_tables = []
    for table in (ahead, back):
        high, low = halves(table)
        inner_tables.append(np.concatenate([high, high, low], axis=0))
    return (
        first_table,
        last_table,
        inner_tables[0],
        inner_tables[1],
        np.cos(turn).astype(np.float32),
        np.sin(turn).astype(np.float32),
    )


def split(values):
    high = values.astype(BF16)
    return high, (values - high.astype(F32)).astype(BF16)


def dot(left, right):
    return jnp.dot(left, right, preferred_element_type=F32)


def kernel(
    n, m, width, scale,
    query_in, key_in, value_in, taps_in, grad_in,
    first_in, last_in, ahead_in, back_in, cos_in, sin_in,
    mixer_out, dquery_out, dkey_out, dvalue_out, dtaps_out,
    mixer_ref, dquery_ref, dkey_ref, dvalue_ref, dtaps_ref,
    query_ref, key_ref, value_ref, taps_ref, grad_ref,
    first_ref, last_ref, ahead_ref, back_ref, cos_ref, sin_ref,
    send1, recv1, send2, recv2, send3, recv3, send4, recv4, send5, recv5,
    stat_out, stat_in, shuffle, query_t, grad_t, conv_t, taps_spec, mixed_spec,
    send_sem, recv_sem, load_sem, store_sem,
):
    loads = [
        pltpu.make_async_copy(source, target, load_sem.at[number])
        for number, (source, target) in enumerate([
            (key_in, key_ref), (value_in, value_ref), (taps_in, taps_ref),
            (query_in, query_ref), (grad_in, grad_ref), (first_in, first_ref),
            (ahead_in, ahead_ref), (back_in, back_ref), (last_in, last_ref),
            (cos_in, cos_ref), (sin_in, sin_ref),
        ])
    ]
    for load in loads:
        load.start()
    mixer_store, dquery_store, dkey_store, dvalue_store, dtaps_store = stores = [
        pltpu.make_async_copy(source, target, store_sem.at[number])
        for number, (source, target) in enumerate([
            (mixer_ref, mixer_out), (dquery_ref, dquery_out), (dkey_ref, dkey_out),
            (dvalue_ref, dvalue_out), (dtaps_ref, dtaps_out),
        ])
    ]
    me = lax.axis_index("ctx")
    mine = lax.axis_index("tp")
    rows, cols = query_ref.shape
    group = cols // n
    chips = n // 4

    barrier = pltpu.get_barrier_semaphore()

    side = me // (2 * chips)
    place = lax.rem(me // 2, chips)
    core = lax.rem(me, 2)

    def partner(step):
        turn = step // 4
        half = lax.rem(turn, 2)
        far = jnp.where(half == 0, chips // 2 + turn // 2, chips // 2 - (turn + 1) // 2)
        far = jnp.where(core == 0, far, chips - far)
        flip = lax.rem(step, 4) // 2
        swap = lax.rem(step, 2)
        return (
            lax.rem(side + flip, 2) * (2 * chips)
            + lax.rem(place + far, chips) * 2
            + lax.rem(core + swap, 2)
        )

    def for_partners(body):
        def step(number, carry):
            body(partner(number))
            return carry

        lax.fori_loop(0, n - 4, step, 0)
        lax.fori_loop(n - 3, n, step, 0)

    def greet_ctx(peer):
        pl.semaphore_signal(barrier, inc=1, device_id=(peer, mine), device_id_type=MESH)

    def greet_tp(step, carry):
        peer = lax.rem(mine + step, m)
        pl.semaphore_signal(barrier, inc=1, device_id=(me, peer), device_id_type=MESH)
        return carry

    for_partners(greet_ctx)
    lax.fori_loop(1, m, greet_tp, 0)

    def exchange(phase, source, target):
        def start(peer):
            pltpu.make_async_remote_copy(
                src_ref=source.at[peer],
                dst_ref=target.at[me],
                send_sem=send_sem.at[phase],
                recv_sem=recv_sem.at[phase],
                device_id=(peer, mine),
                device_id_type=MESH,
            ).start()

        for_partners(start)
        target[me] = source[me]

    def arrived(phase, source, target):
        pltpu.make_async_copy(
            source.at[pl.ds(0, n - 1)], target.at[pl.ds(0, n - 1)], recv_sem.at[phase]
        ).wait()

    def sent(phase, source, target):
        pltpu.make_async_copy(
            source.at[pl.ds(0, n - 1)], target.at[pl.ds(0, n - 1)], send_sem.at[phase]
        ).wait()

    def stage_first(blocks):
        shuffle[...] = blocks.astype(F32).reshape(n * group, rows)
        columns = jnp.concatenate(
            [shuffle[pl.ds(c, n, stride=group), :].astype(BF16) for c in range(group)], axis=1
        )
        outer = dot(first_ref[...], jnp.concatenate([columns, columns], axis=0))
        cos, sin = cos_ref[...], sin_ref[...]
        turned = []
        for c in range(group):
            real = outer[:n, c * rows : (c + 1) * rows]
            imag = outer[n:, c * rows : (c + 1) * rows]
            turned.append(
                jnp.concatenate([real * cos + imag * sin, imag * cos - real * sin], axis=1)
            )
        high, low = split(jnp.concatenate(turned, axis=0))
        return dot(jnp.concatenate([high, low, high], axis=1), ahead_ref[...])

    def stage_last(real, imag):
        high, low = split(jnp.concatenate([real, imag], axis=1))
        inner = dot(jnp.concatenate([high, low, high], axis=1), back_ref[...])
        cos, sin = cos_ref[...], sin_ref[...]
        turned = []
        for c in range(group):
            real = inner[c * n : (c + 1) * n, :rows]
            imag = inner[c * n : (c + 1) * n, rows:]
            turned.append(
                jnp.concatenate([real * cos - imag * sin, real * sin + imag * cos], axis=0)
            )
        high, low = split(jnp.concatenate(turned, axis=1))
        outer = dot(last_ref[...], jnp.concatenate([high, low, high], axis=0))
        for c in range(group):
            shuffle[pl.ds(c, n, stride=group), :] = outer[:, c * rows : (c + 1) * rows] * scale
        return shuffle[...].reshape(n, group, rows)

    for load in loads[:3]:
        load.wait()
    mixed = (key_ref[...].astype(F32) * value_ref[...].astype(F32)).astype(BF16).astype(F32)
    send1[:, :group, :] = mixed.T.reshape(n, group, rows).astype(BF16)
    send1[:, group:, :] = taps_ref[...].astype(F32).T.reshape(n, group, rows).astype(BF16)
    pl.semaphore_wait(barrier, n + m - 2)
    exchange(0, send1, recv1)
    for load in loads[3:]:
        load.wait()
    query_t[...] = query_ref[...].astype(F32).T
    grad_t[...] = grad_ref[...].astype(F32).T
    stat_out[...] = jnp.zeros_like(stat_out)
    arrived(0, send1, recv1)

    mixed_spec[...] = stage_first(recv1[:, :group, :])
    taps_spec[...] = stage_first(recv1[:, group:, :])
    mixed_real, mixed_imag = mixed_spec[:, :rows], mixed_spec[:, rows:]
    taps_real, taps_imag = taps_spec[:, :rows], taps_spec[:, rows:]
    send2[...] = stage_last(
        mixed_real * taps_real - mixed_imag * taps_imag,
        mixed_real * taps_imag + mixed_imag * taps_real,
    ).astype(BF16)
    exchange(1, send2, recv2)
    arrived(1, send2, recv2)

    conv_t[...] = recv2[...].astype(F32).reshape(cols, rows)
    gated = query_t[...] * conv_t[...]
    stat_out[0:1, :] = jnp.sum(gated * gated, axis=0, keepdims=True)
    stat_out[1:2, :] = jnp.sum(grad_t[...] * gated, axis=0, keepdims=True)

    def send_stats(step, carry):
        peer = lax.rem(mine + step, m)
        pltpu.make_async_remote_copy(
            src_ref=stat_out,
            dst_ref=stat_in.at[mine],
            send_sem=send_sem.at[5],
            recv_sem=recv_sem.at[5],
            device_id=(me, peer),
            device_id_type=MESH,
        ).start()
        return carry

    lax.fori_loop(1, m, send_stats, 0)
    stat_in[mine] = stat_out[...]
    pltpu.make_async_copy(
        stat_in.at[pl.ds(0, m - 1)], stat_in.at[pl.ds(0, m - 1)], recv_sem.at[5]
    ).wait()
    totals = jnp.sum(stat_in[...], axis=0)
    inverse_rms = lax.rsqrt(totals[0:1, :] / width + EPS)
    dots = totals[1:2, :] / width
    weight = inverse_rms * inverse_rms * inverse_rms * dots

    gated = query_t[...] * conv_t[...]
    dgated = inverse_rms * grad_t[...] - weight * gated
    send3[...] = (dgated * query_t[...]).astype(BF16).reshape(n, group, rows)
    exchange(2, send3, recv3)
    mixer_ref[...] = (gated * inverse_rms).T.astype(BF16)
    dquery_ref[...] = (dgated * conv_t[...]).T.astype(BF16)
    mixer_store.start()
    dquery_store.start()
    arrived(2, send3, recv3)

    grads = stage_first(recv3[...])
    grads_real, grads_imag = grads[:, :rows], grads[:, rows:]
    taps_real, taps_imag = taps_spec[:, :rows], taps_spec[:, rows:]
    send4[...] = stage_last(
        grads_real * taps_real + grads_imag * taps_imag,
        grads_imag * taps_real - grads_real * taps_imag,
    ).astype(BF16)
    exchange(3, send4, recv4)
    mixed_real, mixed_imag = mixed_spec[:, :rows], mixed_spec[:, rows:]
    send5[...] = stage_last(
        grads_real * mixed_real + grads_imag * mixed_imag,
        grads_imag * mixed_real - grads_real * mixed_imag,
    ).astype(BF16)
    exchange(4, send5, recv5)
    arrived(3, send4, recv4)

    dmixed = recv4[...].astype(F32).reshape(cols, rows).T
    dkey_ref[...] = (dmixed * value_ref[...].astype(F32)).astype(BF16)
    dvalue_ref[...] = (dmixed * key_ref[...].astype(F32)).astype(BF16)
    dkey_store.start()
    dvalue_store.start()
    arrived(4, send5, recv5)
    dtaps_ref[...] = recv5[...].astype(F32).reshape(cols, rows).T.astype(BF16)
    dtaps_store.start()

    sent(0, send1, recv1)
    sent(1, send2, recv2)
    sent(2, send3, recv3)
    sent(3, send4, recv4)
    sent(4, send5, recv5)
    pltpu.make_async_copy(
        stat_in.at[pl.ds(0, m - 1)], stat_in.at[pl.ds(0, m - 1)], send_sem.at[5]
    ).wait()
    for store in stores:
        store.wait()


def store_kernel(*refs):
    sources, targets, middles, load_sem, store_sem = refs[:5], refs[5:10], refs[10:15], *refs[15:]
    loads = [
        pltpu.make_async_copy(sources[k], middles[k], load_sem.at[k]) for k in range(len(sources))
    ]
    stores = [
        pltpu.make_async_copy(middles[k], targets[k], store_sem.at[k]) for k in range(len(sources))
    ]
    for load in loads:
        load.start()
    for load, store in zip(loads, stores, strict=True):
        load.wait()
        store.start()
    for store in stores:
        store.wait()


def per_device(n, m, query, key_proj, value_proj, filter_taps, grad_out):
    rows, cols = query.shape
    group = cols // n
    length = rows * n
    consts = [jnp.asarray(table) for table in tables(n, rows)]
    where = pl.BlockSpec(memory_space=pl.ANY)
    one = pltpu.VMEM((n, group, rows), BF16)
    two = pltpu.VMEM((n, 2 * group, rows), BF16)
    wide = pltpu.VMEM((cols, rows), F32)
    local = pltpu.VMEM((rows, cols), BF16)
    shapes = [jax.ShapeDtypeStruct((rows, cols), BF16)] * 5
    results = pl.pallas_call(
        functools.partial(kernel, n, m, cols * m, 1.0 / (math.sqrt(length) * length)),
        out_shape=shapes,
        in_specs=[where] * 11,
        out_specs=[where] * 5,
        scratch_shapes=[
            local, local, local, local, local,
            local, local, local, local, local,
            *[pltpu.VMEM(table.shape, table.dtype) for table in consts],
            two, two, one, one, one, one, one, one, one, one,
            pltpu.VMEM((8, rows), F32),
            pltpu.VMEM((m, 8, rows), F32),
            pltpu.VMEM((n * group, rows), F32),
            wide, wide, wide,
            pltpu.VMEM((n * group, 2 * rows), F32),
            pltpu.VMEM((n * group, 2 * rows), F32),
            pltpu.SemaphoreType.DMA((6,)),
            pltpu.SemaphoreType.DMA((6,)),
            pltpu.SemaphoreType.DMA((11,)),
            pltpu.SemaphoreType.DMA((5,)),
        ],
        compiler_params=pltpu.CompilerParams(
            collective_id=0, has_side_effects=True, vmem_limit_bytes=VMEM_BYTES
        ),
    )(query, key_proj, value_proj, filter_taps, grad_out, *consts)
    return pl.pallas_call(
        store_kernel,
        out_shape=shapes,
        in_specs=[where] * 5,
        out_specs=[where] * 5,
        scratch_shapes=[local] * 5 + [pltpu.SemaphoreType.DMA((5,))] * 2,
        compiler_params=pltpu.CompilerParams(vmem_limit_bytes=VMEM_BYTES),
    )(*results)


def solution(mesh):
    spec = P("ctx", "tp")
    return jax.shard_map(
        functools.partial(per_device, mesh.shape["ctx"], mesh.shape["tp"]),
        mesh=mesh,
        in_specs=(spec,) * 5,
        out_specs=(spec,) * 5,
        check_vma=False,
    )
```

```python
import functools
import math

import jax
import jax.numpy as jnp
import ml_dtypes
import numpy as np
from jax import lax
from jax.experimental import pallas as pl
from jax.experimental.pallas import tpu as pltpu
from jax.sharding import PartitionSpec as P

MESH = pl.DeviceIdType.MESH
F32 = jnp.float32
BF16 = jnp.bfloat16
EPS = 1e-05
AHEAD = 4
STRIDE = 2
VMEM_BYTES = 63 * 1024 * 1024


def halves(table):
    high = table.astype(ml_dtypes.bfloat16)
    low = (table - high.astype(np.float64)).astype(ml_dtypes.bfloat16)
    return high, low


def tables(blocks, lanes):
    total = blocks * lanes
    i = np.arange(blocks, dtype=np.float64)
    j = np.arange(lanes, dtype=np.float64)
    outer = 2 * np.pi * np.outer(i + 0.25, i) / blocks
    first = np.concatenate([np.cos(outer), -np.sin(outer)], axis=0)
    first_high, first_low = halves(first)
    first_table = np.concatenate([first_high, first_low], axis=1)
    last_high, last_low = halves(np.ascontiguousarray(first.T))
    last_table = np.concatenate([last_high, last_high, last_low], axis=1)
    turn = 2 * np.pi * np.outer(i + 0.25, j) / total
    inner = 2 * np.pi * (np.outer(j, j) % lanes) / lanes
    cos, sin = np.cos(inner), np.sin(inner)
    ahead = np.block([[cos, -sin], [sin, cos]])
    back = np.block([[cos, sin], [-sin, cos]])
    inner_tables = []
    for table in (ahead, back):
        high, low = halves(table)
        inner_tables.append(np.concatenate([high, high, low], axis=0))
    return (
        first_table,
        last_table,
        inner_tables[0],
        inner_tables[1],
        np.cos(turn).astype(np.float32),
        np.sin(turn).astype(np.float32),
    )


def split(values):
    high = values.astype(BF16)
    return high, (values - high.astype(F32)).astype(BF16)


def dot(left, right):
    return jnp.dot(left, right, preferred_element_type=F32)


def kernel(
    n, m, width, scale,
    query_in, key_in, value_in, taps_in, grad_in,
    first_in, last_in, ahead_in, back_in, cos_in, sin_in,
    mixer_ref, dquery_ref, dkey_ref, dvalue_ref, dtaps_ref,
    query_ref, key_ref, value_ref, taps_ref, grad_ref,
    first_ref, last_ref, ahead_ref, back_ref, cos_ref, sin_ref,
    send1, recv1, send2, recv2, send3, recv3, send4, recv4, send5, recv5,
    stat_out, stat_in, shuffle, query_t, grad_t, conv_t, taps_spec, mixed_spec,
    send_sem, recv_sem, load_sem,
):
    loads = [
        pltpu.make_async_copy(source, target, load_sem.at[number])
        for number, (source, target) in enumerate([
            (key_in, key_ref), (value_in, value_ref), (taps_in, taps_ref),
            (query_in, query_ref), (grad_in, grad_ref), (first_in, first_ref),
            (ahead_in, ahead_ref), (back_in, back_ref), (last_in, last_ref),
            (cos_in, cos_ref), (sin_in, sin_ref),
        ])
    ]
    me = lax.axis_index("ctx")
    mine = lax.axis_index("tp")
    rows, cols = query_ref.shape
    group = cols // n
    chips = n // 4

    barrier = pltpu.get_barrier_semaphore()

    side = me // (2 * chips)
    place = lax.rem(me // 2, chips)
    core = lax.rem(me, 2)

    def partner(step):
        turn = step // 4
        half = lax.rem(turn, 2)
        far = jnp.where(half == 0, chips // 2 + turn // 2, chips // 2 - (turn + 1) // 2)
        far = jnp.where(core == 0, far, chips - far)
        flip = lax.rem(step, 4) // 2
        swap = lax.rem(step, 2)
        return (
            lax.rem(side + flip, 2) * (2 * chips)
            + lax.rem(place + far, chips) * 2
            + lax.rem(core + swap, 2)
        )

    def for_partners(body):
        def step(number, carry):
            body(partner(number))
            return carry

        lax.fori_loop(0, n - 4, step, 0)
        lax.fori_loop(n - 3, n, step, 0)

    def greet_ctx(peer):
        pl.semaphore_signal(barrier, inc=1, device_id=(peer, mine), device_id_type=MESH)

    def greet_tp(step, carry):
        peer = lax.rem(mine + step, m)
        pl.semaphore_signal(barrier, inc=1, device_id=(me, peer), device_id_type=MESH)
        return carry

    for_partners(greet_ctx)
    lax.fori_loop(1, m, greet_tp, 0)
    for load in loads:
        load.start()

    def start(phase, source, target, peer):
        pltpu.make_async_remote_copy(
            src_ref=source.at[peer],
            dst_ref=target.at[me],
            send_sem=send_sem.at[phase],
            recv_sem=recv_sem.at[phase],
            device_id=(peer, mine),
            device_id_type=MESH,
        ).start()

    def exchange(phase, source, target):
        for_partners(functools.partial(start, phase, source, target))
        target[me] = source[me]

    def deliver(phase, source, target, first, last):
        def step(number, carry):
            flip = lax.rem(number, 4) // 2
            swap = lax.rem(number, 2)
            peer = (
                lax.rem(side + flip, 2) * (2 * chips)
                + (number // 4) * 2
                + lax.rem(core + swap, 2)
            )

            @pl.when(peer != me)
            def _():
                start(phase, source, target, peer)

            return carry

        lax.fori_loop(4 * first, 4 * last, step, 0)

    def arrived(phase, source, target):
        pltpu.make_async_copy(
            source.at[pl.ds(0, n - 1)], target.at[pl.ds(0, n - 1)], recv_sem.at[phase]
        ).wait()

    def sent(phase, source, target):
        pltpu.make_async_copy(
            source.at[pl.ds(0, n - 1)], target.at[pl.ds(0, n - 1)], send_sem.at[phase]
        ).wait()

    def stage_first(blocks):
        shuffle[...] = blocks.astype(F32).reshape(n * group, rows)
        columns = jnp.concatenate(
            [shuffle[pl.ds(c, n, stride=group), :].astype(BF16) for c in range(group)], axis=1
        )
        outer = dot(first_ref[...], jnp.concatenate([columns, columns], axis=0))
        cos, sin = cos_ref[...], sin_ref[...]
        turned = []
        for c in range(group):
            real = outer[:n, c * rows : (c + 1) * rows]
            imag = outer[n:, c * rows : (c + 1) * rows]
            turned.append(
                jnp.concatenate([real * cos + imag * sin, imag * cos - real * sin], axis=1)
            )
        high, low = split(jnp.concatenate(turned, axis=0))
        return dot(jnp.concatenate([high, low, high], axis=1), ahead_ref[...])

    def stage_last(real, imag):
        high, low = split(jnp.concatenate([real, imag], axis=1))
        inner = dot(jnp.concatenate([high, low, high], axis=1), back_ref[...])
        cos, sin = cos_ref[...], sin_ref[...]
        turned = []
        for c in range(group):
            real = inner[c * n : (c + 1) * n, :rows]
            imag = inner[c * n : (c + 1) * n, rows:]
            turned.append(
                jnp.concatenate([real * cos - imag * sin, real * sin + imag * cos], axis=0)
            )
        high, low = split(jnp.concatenate(turned, axis=1))
        outer = dot(last_ref[...], jnp.concatenate([high, low, high], axis=0))
        for c in range(group):
            shuffle[pl.ds(c, n, stride=group), :] = outer[:, c * rows : (c + 1) * rows] * scale
        return shuffle[...].reshape(n, group, rows)

    for load in loads[:3]:
        load.wait()
    mixed = (key_ref[...].astype(F32) * value_ref[...].astype(F32)).astype(BF16).astype(F32)
    send1[:, :group, :] = mixed.T.reshape(n, group, rows).astype(BF16)
    send1[:, group:, :] = taps_ref[...].astype(F32).T.reshape(n, group, rows).astype(BF16)
    pl.semaphore_wait(barrier, n + m - 2)
    exchange(0, send1, recv1)
    for load in loads[3:]:
        load.wait()
    query_t[...] = query_ref[...].astype(F32).T
    grad_t[...] = grad_ref[...].astype(F32).T
    stat_out[...] = jnp.zeros_like(stat_out)
    arrived(0, send1, recv1)

    mixed_spec[...] = stage_first(recv1[:, :group, :])
    taps_spec[...] = stage_first(recv1[:, group:, :])
    mixed_real, mixed_imag = mixed_spec[:, :rows], mixed_spec[:, rows:]
    taps_real, taps_imag = taps_spec[:, :rows], taps_spec[:, rows:]
    send2[...] = stage_last(
        mixed_real * taps_real - mixed_imag * taps_imag,
        mixed_real * taps_imag + mixed_imag * taps_real,
    ).astype(BF16)
    exchange(1, send2, recv2)
    arrived(1, send2, recv2)

    conv_t[...] = recv2[...].astype(F32).reshape(cols, rows)
    gated = query_t[...] * conv_t[...]
    stat_out[0:1, :] = jnp.sum(gated * gated, axis=0, keepdims=True)
    stat_out[1:2, :] = jnp.sum(grad_t[...] * gated, axis=0, keepdims=True)

    def send_stats(step, carry):
        peer = lax.rem(mine + step, m)
        pltpu.make_async_remote_copy(
            src_ref=stat_out,
            dst_ref=stat_in.at[mine],
            send_sem=send_sem.at[5],
            recv_sem=recv_sem.at[5],
            device_id=(me, peer),
            device_id_type=MESH,
        ).start()
        return carry

    lax.fori_loop(1, m, send_stats, 0)
    stat_in[mine] = stat_out[...]
    pltpu.make_async_copy(
        stat_in.at[pl.ds(0, m - 1)], stat_in.at[pl.ds(0, m - 1)], recv_sem.at[5]
    ).wait()
    totals = jnp.sum(stat_in[...], axis=0)
    inverse_rms = lax.rsqrt(totals[0:1, :] / width + EPS)
    dots = totals[1:2, :] / width
    weight = inverse_rms * inverse_rms * inverse_rms * dots

    gated = query_t[...] * conv_t[...]
    dgated = inverse_rms * grad_t[...] - weight * gated
    send3[...] = (dgated * query_t[...]).astype(BF16).reshape(n, group, rows)
    exchange(2, send3, recv3)
    mixer_ref[...] = (gated * inverse_rms).T.astype(BF16)
    dquery_ref[...] = (dgated * conv_t[...]).T.astype(BF16)
    arrived(2, send3, recv3)

    grads = stage_first(recv3[...])
    grads_real, grads_imag = grads[:, :rows], grads[:, rows:]
    taps_real, taps_imag = taps_spec[:, :rows], taps_spec[:, rows:]
    send4[...] = stage_last(
        grads_real * taps_real + grads_imag * taps_imag,
        grads_imag * taps_real - grads_real * taps_imag,
    ).astype(BF16)
    deliver(3, send4, recv4, 0, AHEAD)
    recv4[me] = send4[me]
    mixed_real, mixed_imag = mixed_spec[:, :rows], mixed_spec[:, rows:]
    send5[...] = stage_last(
        grads_real * mixed_real + grads_imag * mixed_imag,
        grads_imag * mixed_real - grads_real * mixed_imag,
    ).astype(BF16)
    deliver(4, send5, recv5, 0, AHEAD)
    recv5[me] = send5[me]
    for first in range(AHEAD, chips, STRIDE):
        deliver(3, send4, recv4, first, min(first + STRIDE, chips))
        deliver(4, send5, recv5, first, min(first + STRIDE, chips))
    arrived(3, send4, recv4)

    dmixed = recv4[...].astype(F32).reshape(cols, rows).T
    dkey_ref[...] = (dmixed * value_ref[...].astype(F32)).astype(BF16)
    dvalue_ref[...] = (dmixed * key_ref[...].astype(F32)).astype(BF16)
    arrived(4, send5, recv5)
    dtaps_ref[...] = recv5[...].astype(F32).reshape(cols, rows).T.astype(BF16)

    sent(0, send1, recv1)
    sent(1, send2, recv2)
    sent(2, send3, recv3)
    sent(3, send4, recv4)
    sent(4, send5, recv5)
    pltpu.make_async_copy(
        stat_in.at[pl.ds(0, m - 1)], stat_in.at[pl.ds(0, m - 1)], send_sem.at[5]
    ).wait()


def store_kernel(*refs):
    sources, targets, sem = refs[:5], refs[5:10], refs[10]
    stores = [
        pltpu.make_async_copy(source, target, sem.at[number])
        for number, (source, target) in enumerate(zip(sources, targets, strict=True))
    ]
    for store in stores:
        store.start()
    for store in stores:
        store.wait()


def per_device(n, m, query, key_proj, value_proj, filter_taps, grad_out):
    rows, cols = query.shape
    group = cols // n
    length = rows * n
    consts = [jnp.asarray(table) for table in tables(n, rows)]
    where = pl.BlockSpec(memory_space=pl.ANY)
    one = pltpu.VMEM((n, group, rows), BF16)
    two = pltpu.VMEM((n, 2 * group, rows), BF16)
    wide = pltpu.VMEM((cols, rows), F32)
    local = pltpu.VMEM((rows, cols), BF16)
    shapes = [jax.ShapeDtypeStruct((rows, cols), BF16)] * 5
    results = pl.pallas_call(
        functools.partial(kernel, n, m, cols * m, 1.0 / (math.sqrt(length) * length)),
        out_shape=[pltpu.VMEM((rows, cols), BF16)] * 5,
        in_specs=[where] * 11,
        out_specs=[pl.BlockSpec(memory_space=pltpu.VMEM)] * 5,
        scratch_shapes=[
            local, local, local, local, local,
            *[pltpu.VMEM(table.shape, table.dtype) for table in consts],
            two, two, one, one, one, one, one, one, one, one,
            pltpu.VMEM((8, rows), F32),
            pltpu.VMEM((m, 8, rows), F32),
            pltpu.VMEM((n * group, rows), F32),
            wide, wide, wide,
            pltpu.VMEM((n * group, 2 * rows), F32),
            pltpu.VMEM((n * group, 2 * rows), F32),
            pltpu.SemaphoreType.DMA((6,)),
            pltpu.SemaphoreType.DMA((6,)),
            pltpu.SemaphoreType.DMA((11,)),
        ],
        compiler_params=pltpu.CompilerParams(
            collective_id=0, has_side_effects=True, vmem_limit_bytes=VMEM_BYTES
        ),
    )(query, key_proj, value_proj, filter_taps, grad_out, *consts)
    return pl.pallas_call(
        store_kernel,
        out_shape=shapes,
        in_specs=[pl.BlockSpec(memory_space=pltpu.VMEM)] * 5,
        out_specs=[where] * 5,
        scratch_shapes=[pltpu.SemaphoreType.DMA((5,))],
        compiler_params=pltpu.CompilerParams(vmem_limit_bytes=8 * 1024 * 1024),
    )(*results)


def solution(mesh):
    spec = P("ctx", "tp")
    return jax.shard_map(
        functools.partial(per_device, mesh.shape["ctx"], mesh.shape["tp"]),
        mesh=mesh,
        in_specs=(spec,) * 5,
        out_specs=(spec,) * 5,
        check_vma=False,
    )
```

```python
import functools
import math

import jax
import jax.numpy as jnp
import ml_dtypes
import numpy as np
from jax import lax
from jax.experimental import pallas as pl
from jax.experimental.pallas import tpu as pltpu
from jax.sharding import PartitionSpec as P

MESH = pl.DeviceIdType.MESH
F32 = jnp.float32
BF16 = jnp.bfloat16
EPS = 1e-05
AHEAD = 4
STRIDE = 2
VMEM_BYTES = 63 * 1024 * 1024


def halves(table):
    high = table.astype(ml_dtypes.bfloat16)
    low = (table - high.astype(np.float64)).astype(ml_dtypes.bfloat16)
    return high, low


def tables(blocks, lanes):
    total = blocks * lanes
    i = np.arange(blocks, dtype=np.float64)
    j = np.arange(lanes, dtype=np.float64)
    outer = 2 * np.pi * np.outer(i + 0.25, i) / blocks
    first = np.concatenate([np.cos(outer), -np.sin(outer)], axis=0)
    first_high, first_low = halves(first)
    first_table = np.concatenate([first_high, first_low], axis=1)
    last_high, last_low = halves(np.ascontiguousarray(first.T))
    last_table = np.concatenate([last_high, last_high, last_low], axis=1)
    turn = 2 * np.pi * np.outer(i + 0.25, j) / total
    inner = 2 * np.pi * (np.outer(j, j) % lanes) / lanes
    cos, sin = np.cos(inner), np.sin(inner)
    ahead = np.block([[cos, -sin], [sin, cos]])
    back = np.block([[cos, sin], [-sin, cos]])
    inner_tables = []
    for table in (ahead, back):
        high, low = halves(table)
        inner_tables.append(np.concatenate([high, high, low], axis=0))
    return (
        first_table,
        last_table,
        inner_tables[0],
        inner_tables[1],
        np.cos(turn).astype(np.float32),
        np.sin(turn).astype(np.float32),
    )


def split(values):
    high = values.astype(BF16)
    return high, (values - high.astype(F32)).astype(BF16)


def dot(left, right):
    return jnp.dot(left, right, preferred_element_type=F32)


def kernel(
    n, m, width, scale,
    query_in, key_in, value_in, taps_in, grad_in,
    first_in, last_in, ahead_in, back_in, cos_in, sin_in,
    mixer_ref, dquery_ref, dkey_ref, dvalue_ref, dtaps_ref,
    query_ref, key_ref, value_ref, taps_ref, grad_ref,
    first_ref, last_ref, ahead_ref, back_ref, cos_ref, sin_ref,
    send1a, send1b, recv1a, recv1b, send2a, send2b, recv2a, recv2b,
    send3a, send3b, recv3a, recv3b, send4, recv4, send5, recv5,
    stat_out, stat_in, shuffle, query_t, grad_t, conv_t, taps_spec, mixed_spec,
    send_sem, recv_sem, load_sem,
):
    loads = [
        pltpu.make_async_copy(source, target, load_sem.at[number])
        for number, (source, target) in enumerate([
            (key_in, key_ref), (value_in, value_ref), (taps_in, taps_ref),
            (query_in, query_ref), (grad_in, grad_ref), (first_in, first_ref),
            (ahead_in, ahead_ref), (back_in, back_ref), (last_in, last_ref),
            (cos_in, cos_ref), (sin_in, sin_ref),
        ])
    ]
    me = lax.axis_index("ctx")
    mine = lax.axis_index("tp")
    rows, cols = query_ref.shape
    group = cols // n
    chips = n // 4

    barrier = pltpu.get_barrier_semaphore()

    side = me // (2 * chips)
    place = lax.rem(me // 2, chips)
    core = lax.rem(me, 2)

    seats = [
        lax.rem(side + flip, 2) * (2 * chips) + lax.rem(core + swap, 2)
        for flip in range(2)
        for swap in range(2)
    ]

    def for_partners(body):
        def turn_step(turn, carry):
            half = lax.rem(turn, 2)
            far = jnp.where(half == 0, chips // 2 + turn // 2, chips // 2 - (turn + 1) // 2)
            far = jnp.where(core == 0, far, chips - far)
            there = 2 * lax.rem(place + far, chips)
            for seat in seats:
                body(seat + there)
            return carry

        lax.fori_loop(0, chips - 1, turn_step, 0)
        for seat in seats[1:]:
            body(seat + 2 * place)

    def greet_ctx(peer):
        pl.semaphore_signal(barrier, inc=1, device_id=(peer, mine), device_id_type=MESH)

    def greet_tp(step, carry):
        peer = lax.rem(mine + step, m)
        pl.semaphore_signal(barrier, inc=1, device_id=(me, peer), device_id_type=MESH)
        return carry

    for_partners(greet_ctx)
    lax.fori_loop(1, m, greet_tp, 0)
    for load in loads:
        load.start()

    def start(phase, source, target, peer):
        pltpu.make_async_remote_copy(
            src_ref=source.at[peer],
            dst_ref=target.at[me],
            send_sem=send_sem.at[phase],
            recv_sem=recv_sem.at[phase],
            device_id=(peer, mine),
            device_id_type=MESH,
        ).start()

    def exchange(phase, source, target):
        for_partners(functools.partial(start, phase, source, target))
        target[me] = source[me]

    def deliver(phase, source, target, first, last):
        def step(there, carry):
            for seat in seats[1:]:
                start(phase, source, target, seat + 2 * there)

            @pl.when(there != place)
            def _():
                start(phase, source, target, seats[0] + 2 * there)

            return carry

        lax.fori_loop(first, last, step, 0)

    def arrived(phase, source, target):
        pltpu.make_async_copy(
            source.at[pl.ds(0, n - 1)], target.at[pl.ds(0, n - 1)], recv_sem.at[phase]
        ).wait()

    def sent(phase, source, target):
        pltpu.make_async_copy(
            source.at[pl.ds(0, n - 1)], target.at[pl.ds(0, n - 1)], send_sem.at[phase]
        ).wait()

    def stage_first(blocks):
        count = blocks.shape[1]
        shuffle[pl.ds(0, n * count), :] = blocks.astype(F32).reshape(n * count, rows)
        columns = jnp.concatenate(
            [shuffle[pl.ds(c, n, stride=count), :].astype(BF16) for c in range(count)], axis=1
        )
        outer = dot(first_ref[...], jnp.concatenate([columns, columns], axis=0))
        cos, sin = cos_ref[...], sin_ref[...]
        turned = []
        for c in range(count):
            real = outer[:n, c * rows : (c + 1) * rows]
            imag = outer[n:, c * rows : (c + 1) * rows]
            turned.append(
                jnp.concatenate([real * cos + imag * sin, imag * cos - real * sin], axis=1)
            )
        high, low = split(jnp.concatenate(turned, axis=0))
        return dot(jnp.concatenate([high, low, high], axis=1), ahead_ref[...])

    def stage_last(real, imag):
        count = real.shape[0] // n
        high, low = split(jnp.concatenate([real, imag], axis=1))
        inner = dot(jnp.concatenate([high, low, high], axis=1), back_ref[...])
        cos, sin = cos_ref[...], sin_ref[...]
        turned = []
        for c in range(count):
            real = inner[c * n : (c + 1) * n, :rows]
            imag = inner[c * n : (c + 1) * n, rows:]
            turned.append(
                jnp.concatenate([real * cos - imag * sin, real * sin + imag * cos], axis=0)
            )
        high, low = split(jnp.concatenate(turned, axis=1))
        outer = dot(last_ref[...], jnp.concatenate([high, low, high], axis=0))
        for c in range(count):
            shuffle[pl.ds(c, n, stride=count), :] = outer[:, c * rows : (c + 1) * rows] * scale
        return shuffle[pl.ds(0, n * count), :].reshape(n, count, rows)

    for load in loads[:3]:
        load.wait()
    half = group // 2
    mixed = (key_ref[...].astype(F32) * value_ref[...].astype(F32)).astype(BF16).astype(F32)
    mixed = mixed.T.reshape(n, group, rows)
    taps = taps_ref[...].astype(F32).T.reshape(n, group, rows)
    for part, send1 in enumerate((send1a, send1b)):
        chosen = slice(part * half, (part + 1) * half)
        send1[...] = jnp.concatenate([mixed[:, chosen], taps[:, chosen]], axis=1).astype(BF16)
    pl.semaphore_wait(barrier, n + m - 2)
    exchange(0, send1a, recv1a)
    exchange(5, send1b, recv1b)
    for load in loads[3:]:
        load.wait()
    query_t[...] = query_ref[...].astype(F32).T
    grad_t[...] = grad_ref[...].astype(F32).T
    stat_out[...] = jnp.zeros_like(stat_out)

    for part, (phase1, send1, recv1, phase2, send2, recv2) in enumerate((
        (0, send1a, recv1a, 1, send2a, recv2a),
        (5, send1b, recv1b, 6, send2b, recv2b),
    )):
        arrived(phase1, send1, recv1)
        spec = stage_first(recv1[...])
        block = pl.ds(part * half * n, half * n)
        mixed_spec[block, :] = spec[: half * n]
        taps_spec[block, :] = spec[half * n :]
        mixed_real, mixed_imag = spec[: half * n, :rows], spec[: half * n, rows:]
        taps_real, taps_imag = spec[half * n :, :rows], spec[half * n :, rows:]
        send2[...] = stage_last(
            mixed_real * taps_real - mixed_imag * taps_imag,
            mixed_real * taps_imag + mixed_imag * taps_real,
        ).astype(BF16)
        exchange(phase2, send2, recv2)
    arrived(1, send2a, recv2a)
    conv_first = recv2a[...].astype(F32)
    arrived(6, send2b, recv2b)
    conv_t[...] = jnp.concatenate([conv_first, recv2b[...].astype(F32)], axis=1).reshape(
        cols, rows
    )

    gated = query_t[...] * conv_t[...]
    stat_out[0:1, :] = jnp.sum(gated * gated, axis=0, keepdims=True)
    stat_out[1:2, :] = jnp.sum(grad_t[...] * gated, axis=0, keepdims=True)

    def send_stats(step, carry):
        peer = lax.rem(mine + step, m)
        pltpu.make_async_remote_copy(
            src_ref=stat_out,
            dst_ref=stat_in.at[mine],
            send_sem=send_sem.at[7],
            recv_sem=recv_sem.at[7],
            device_id=(me, peer),
            device_id_type=MESH,
        ).start()
        return carry

    lax.fori_loop(1, m, send_stats, 0)
    stat_in[mine] = stat_out[...]
    pltpu.make_async_copy(
        stat_in.at[pl.ds(0, m - 1)], stat_in.at[pl.ds(0, m - 1)], recv_sem.at[7]
    ).wait()
    totals = jnp.sum(stat_in[...], axis=0)
    inverse_rms = lax.rsqrt(totals[0:1, :] / width + EPS)
    dots = totals[1:2, :] / width
    weight = inverse_rms * inverse_rms * inverse_rms * dots

    gated = query_t[...] * conv_t[...]
    dgated = inverse_rms * grad_t[...] - weight * gated
    gconv = (dgated * query_t[...]).reshape(n, group, rows)
    send3a[...] = gconv[:, :half].astype(BF16)
    exchange(2, send3a, recv3a)
    send3b[...] = gconv[:, half:].astype(BF16)
    exchange(8, send3b, recv3b)
    mixer_ref[...] = (gated * inverse_rms).T.astype(BF16)
    dquery_ref[...] = (dgated * conv_t[...]).T.astype(BF16)

    for part, (phase3, send3, recv3, phase4, send, recv) in enumerate((
        (2, send3a, recv3a, 3, send4, recv4),
        (8, send3b, recv3b, 4, send5, recv5),
    )):
        arrived(phase3, send3, recv3)
        grads = stage_first(recv3[...])
        grads = jnp.concatenate([grads, grads], axis=0)
        block = pl.ds(part * half * n, half * n)
        others = jnp.concatenate([taps_spec[block, :], mixed_spec[block, :]], axis=0)
        grads_real, grads_imag = grads[:, :rows], grads[:, rows:]
        other_real, other_imag = others[:, :rows], others[:, rows:]
        send[...] = stage_last(
            grads_real * other_real + grads_imag * other_imag,
            grads_imag * other_real - grads_real * other_imag,
        ).astype(BF16)
        deliver(phase4, send, recv, 0, AHEAD)
        recv[me] = send[me]
    for first in range(AHEAD, chips, STRIDE):
        deliver(3, send4, recv4, first, min(first + STRIDE, chips))
        deliver(4, send5, recv5, first, min(first + STRIDE, chips))
    arrived(3, send4, recv4)
    arrived(4, send5, recv5)

    dmixed = jnp.concatenate([recv4[:, :half, :], recv5[:, :half, :]], axis=1)
    dmixed = dmixed.astype(F32).reshape(cols, rows).T
    dkey_ref[...] = (dmixed * value_ref[...].astype(F32)).astype(BF16)
    dvalue_ref[...] = (dmixed * key_ref[...].astype(F32)).astype(BF16)
    dtaps = jnp.concatenate([recv4[:, half:, :], recv5[:, half:, :]], axis=1)
    dtaps_ref[...] = dtaps.astype(F32).reshape(cols, rows).T.astype(BF16)

    sent(0, send1a, recv1a)
    sent(5, send1b, recv1b)
    sent(1, send2a, recv2a)
    sent(6, send2b, recv2b)
    sent(2, send3a, recv3a)
    sent(8, send3b, recv3b)
    sent(3, send4, recv4)
    sent(4, send5, recv5)
    pltpu.make_async_copy(
        stat_in.at[pl.ds(0, m - 1)], stat_in.at[pl.ds(0, m - 1)], send_sem.at[7]
    ).wait()


def store_kernel(*refs):
    sources, targets, sem = refs[:5], refs[5:10], refs[10]
    stores = [
        pltpu.make_async_copy(source, target, sem.at[number])
        for number, (source, target) in enumerate(zip(sources, targets, strict=True))
    ]
    for store in stores:
        store.start()
    for store in stores:
        store.wait()


def per_device(n, m, query, key_proj, value_proj, filter_taps, grad_out):
    rows, cols = query.shape
    group = cols // n
    length = rows * n
    consts = [jnp.asarray(table) for table in tables(n, rows)]
    where = pl.BlockSpec(memory_space=pl.ANY)
    one = pltpu.VMEM((n, group, rows), BF16)
    part = pltpu.VMEM((n, group // 2, rows), BF16)
    wide = pltpu.VMEM((cols, rows), F32)
    local = pltpu.VMEM((rows, cols), BF16)
    shapes = [jax.ShapeDtypeStruct((rows, cols), BF16)] * 5
    results = pl.pallas_call(
        functools.partial(kernel, n, m, cols * m, 1.0 / (math.sqrt(length) * length)),
        out_shape=[pltpu.VMEM((rows, cols), BF16)] * 5,
        in_specs=[where] * 11,
        out_specs=[pl.BlockSpec(memory_space=pltpu.VMEM)] * 5,
        scratch_shapes=[
            local, local, local, local, local,
            *[pltpu.VMEM(table.shape, table.dtype) for table in consts],
            one, one, one, one, part, part, part, part, part, part, part, part, one, one, one, one,
            pltpu.VMEM((8, rows), F32),
            pltpu.VMEM((m, 8, rows), F32),
            pltpu.VMEM((n * group, rows), F32),
            wide, wide, wide,
            pltpu.VMEM((n * group, 2 * rows), F32),
            pltpu.VMEM((n * group, 2 * rows), F32),
            pltpu.SemaphoreType.DMA((9,)),
            pltpu.SemaphoreType.DMA((9,)),
            pltpu.SemaphoreType.DMA((11,)),
        ],
        compiler_params=pltpu.CompilerParams(
            collective_id=0, has_side_effects=True, vmem_limit_bytes=VMEM_BYTES
        ),
    )(query, key_proj, value_proj, filter_taps, grad_out, *consts)
    return pl.pallas_call(
        store_kernel,
        out_shape=shapes,
        in_specs=[pl.BlockSpec(memory_space=pltpu.VMEM)] * 5,
        out_specs=[where] * 5,
        scratch_shapes=[pltpu.SemaphoreType.DMA((5,))],
        compiler_params=pltpu.CompilerParams(vmem_limit_bytes=8 * 1024 * 1024),
    )(*results)


def solution(mesh):
    spec = P("ctx", "tp")
    return jax.shard_map(
        functools.partial(per_device, mesh.shape["ctx"], mesh.shape["tp"]),
        mesh=mesh,
        in_specs=(spec,) * 5,
        out_specs=(spec,) * 5,
        check_vma=False,
    )
```

```python
import functools
import math

import jax
import jax.numpy as jnp
import ml_dtypes
import numpy as np
from jax import lax
from jax.experimental import pallas as pl
from jax.experimental.pallas import tpu as pltpu
from jax.sharding import PartitionSpec as P

MESH = pl.DeviceIdType.MESH
F32 = jnp.float32
BF16 = jnp.bfloat16
EPS = 1e-05
PARTS = (4, 4)
AHEAD = 4
STRIDE = 2
VMEM_BYTES = 63 * 1024 * 1024


def halves(table):
    high = table.astype(ml_dtypes.bfloat16)
    low = (table - high.astype(np.float64)).astype(ml_dtypes.bfloat16)
    return high, low


def tables(blocks, lanes):
    total = blocks * lanes
    i = np.arange(blocks, dtype=np.float64)
    j = np.arange(lanes, dtype=np.float64)
    outer = 2 * np.pi * np.outer(i + 0.25, i) / blocks
    first = np.concatenate([np.cos(outer), -np.sin(outer)], axis=0)
    first_high, first_low = halves(first)
    first_table = np.concatenate([first_high, first_low], axis=1)
    last_high, last_low = halves(np.ascontiguousarray(first.T))
    last_table = np.concatenate([last_high, last_high, last_low], axis=1)
    turn = 2 * np.pi * np.outer(i + 0.25, j) / total
    inner = 2 * np.pi * (np.outer(j, j) % lanes) / lanes
    cos, sin = np.cos(inner), np.sin(inner)
    ahead = np.block([[cos, -sin], [sin, cos]])
    back = np.block([[cos, sin], [-sin, cos]])
    inner_tables = []
    for table in (ahead, back):
        high, low = halves(table)
        inner_tables.append(np.concatenate([high, high, low], axis=0))
    return (
        first_table,
        last_table,
        inner_tables[0],
        inner_tables[1],
        np.cos(turn).astype(np.float32),
        np.sin(turn).astype(np.float32),
    )


def split(values):
    high = values.astype(BF16)
    return high, (values - high.astype(F32)).astype(BF16)


def dot(left, right):
    return jnp.dot(left, right, preferred_element_type=F32)


def kernel(
    n, m, parts, width, scale,
    query_in, key_in, value_in, taps_in, grad_in,
    first_in, last_in, ahead_in, back_in, cos_in, sin_in,
    mixer_ref, dquery_ref, dkey_ref, dvalue_ref, dtaps_ref,
    query_ref, key_ref, value_ref, taps_ref, grad_ref,
    first_ref, last_ref, ahead_ref, back_ref, cos_ref, sin_ref,
    buffers,
    stat_out, stat_in, shuffle, query_t, grad_t, conv_t, taps_spec, mixed_spec,
    send_sem, recv_sem, load_sem,
):
    loads = [
        pltpu.make_async_copy(source, target, load_sem.at[number])
        for number, (source, target) in enumerate([
            (key_in, key_ref), (value_in, value_ref), (taps_in, taps_ref),
            (query_in, query_ref), (grad_in, grad_ref), (first_in, first_ref),
            (ahead_in, ahead_ref), (back_in, back_ref), (last_in, last_ref),
            (cos_in, cos_ref), (sin_in, sin_ref),
        ])
    ]
    me = lax.axis_index("ctx")
    mine = lax.axis_index("tp")
    rows, cols = query_ref.shape
    group = cols // n
    chips = n // 4

    barrier = pltpu.get_barrier_semaphore()

    side = me // (2 * chips)
    place = lax.rem(me // 2, chips)
    core = lax.rem(me, 2)

    seats = [
        lax.rem(side + flip, 2) * (2 * chips) + lax.rem(core + swap, 2)
        for flip in range(2)
        for swap in range(2)
    ]

    def for_partners(body):
        def turn_step(turn, carry):
            half = lax.rem(turn, 2)
            far = jnp.where(half == 0, chips // 2 + turn // 2, chips // 2 - (turn + 1) // 2)
            far = jnp.where(core == 0, far, chips - far)
            there = 2 * lax.rem(place + far, chips)
            for seat in seats:
                body(seat + there)
            return carry

        lax.fori_loop(0, chips - 1, turn_step, 0)
        for seat in seats[1:]:
            body(seat + 2 * place)

    def greet_ctx(peer):
        pl.semaphore_signal(barrier, inc=1, device_id=(peer, mine), device_id_type=MESH)

    def greet_tp(step, carry):
        peer = lax.rem(mine + step, m)
        pl.semaphore_signal(barrier, inc=1, device_id=(me, peer), device_id_type=MESH)
        return carry

    for_partners(greet_ctx)
    lax.fori_loop(1, m, greet_tp, 0)
    for load in loads:
        load.start()

    def start(phase, source, target, peer):
        pltpu.make_async_remote_copy(
            src_ref=source.at[peer],
            dst_ref=target.at[me],
            send_sem=send_sem.at[phase],
            recv_sem=recv_sem.at[phase],
            device_id=(peer, mine),
            device_id_type=MESH,
        ).start()

    def exchange(phase, source, target):
        for_partners(functools.partial(start, phase, source, target))
        target[me] = source[me]

    def deliver(phase, source, target, first, last):
        def step(there, carry):
            for seat in seats[1:]:
                start(phase, source, target, seat + 2 * there)

            @pl.when(there != place)
            def _():
                start(phase, source, target, seats[0] + 2 * there)

            return carry

        lax.fori_loop(first, last, step, 0)

    def arrived(phase, source, target):
        pltpu.make_async_copy(
            source.at[pl.ds(0, n - 1)], target.at[pl.ds(0, n - 1)], recv_sem.at[phase]
        ).wait()

    def sent(phase, source, target):
        pltpu.make_async_copy(
            source.at[pl.ds(0, n - 1)], target.at[pl.ds(0, n - 1)], send_sem.at[phase]
        ).wait()

    def stage_first(blocks):
        count = blocks.shape[1]
        shuffle[pl.ds(0, n * count), :] = blocks.astype(F32).reshape(n * count, rows)
        columns = jnp.concatenate(
            [shuffle[pl.ds(c, n, stride=count), :].astype(BF16) for c in range(count)], axis=1
        )
        outer = dot(first_ref[...], jnp.concatenate([columns, columns], axis=0))
        cos, sin = cos_ref[...], sin_ref[...]
        turned = []
        for c in range(count):
            real = outer[:n, c * rows : (c + 1) * rows]
            imag = outer[n:, c * rows : (c + 1) * rows]
            turned.append(
                jnp.concatenate([real * cos + imag * sin, imag * cos - real * sin], axis=1)
            )
        high, low = split(jnp.concatenate(turned, axis=0))
        return dot(jnp.concatenate([high, low, high], axis=1), ahead_ref[...])

    def stage_last(real, imag):
        count = real.shape[0] // n
        high, low = split(jnp.concatenate([real, imag], axis=1))
        inner = dot(jnp.concatenate([high, low, high], axis=1), back_ref[...])
        cos, sin = cos_ref[...], sin_ref[...]
        turned = []
        for c in range(count):
            real = inner[c * n : (c + 1) * n, :rows]
            imag = inner[c * n : (c + 1) * n, rows:]
            turned.append(
                jnp.concatenate([real * cos - imag * sin, real * sin + imag * cos], axis=0)
            )
        high, low = split(jnp.concatenate(turned, axis=1))
        outer = dot(last_ref[...], jnp.concatenate([high, low, high], axis=0))
        for c in range(count):
            shuffle[pl.ds(c, n, stride=count), :] = outer[:, c * rows : (c + 1) * rows] * scale
        return shuffle[pl.ds(0, n * count), :].reshape(n, count, rows)

    pieces = []
    at = 0
    for number, count in enumerate(parts):
        phases = [
            (4 * number + step, buffers[8 * number + 2 * step], buffers[8 * number + 2 * step + 1])
            for step in range(4)
        ]
        pieces.append((slice(at * n, (at + count) * n), count, phases))
        at += count

    for load in loads[:3]:
        load.wait()
    mixed = (key_ref[...].astype(F32) * value_ref[...].astype(F32)).astype(BF16).astype(F32).T
    taps = taps_ref[...].astype(F32).T
    for rows_here, count, phases in pieces:
        block = (n, count, rows)
        phases[0][1][...] = jnp.concatenate(
            [mixed[rows_here].reshape(block), taps[rows_here].reshape(block)], axis=1
        ).astype(BF16)
    pl.semaphore_wait(barrier, n + m - 2)
    for _, _, phases in pieces:
        exchange(*phases[0])
    for load in loads[3:]:
        load.wait()
    query_t[...] = query_ref[...].astype(F32).T
    grad_t[...] = grad_ref[...].astype(F32).T
    stat_out[...] = jnp.zeros_like(stat_out)

    for rows_here, count, phases in pieces:
        arrived(*phases[0])
        spec = stage_first(phases[0][2][...])
        mixed_here, taps_here = spec[: count * n], spec[count * n :]
        mixed_spec[rows_here, :] = mixed_here
        taps_spec[rows_here, :] = taps_here
        mixed_real, mixed_imag = mixed_here[:, :rows], mixed_here[:, rows:]
        taps_real, taps_imag = taps_here[:, :rows], taps_here[:, rows:]
        phases[1][1][...] = stage_last(
            mixed_real * taps_real - mixed_imag * taps_imag,
            mixed_real * taps_imag + mixed_imag * taps_real,
        ).astype(BF16)
        exchange(*phases[1])

    square_sum = jnp.zeros((1, rows), F32)
    dot_sum = jnp.zeros((1, rows), F32)
    for rows_here, count, phases in pieces:
        arrived(*phases[1])
        conv_here = phases[1][2][...].astype(F32).reshape(n * count, rows)
        conv_t[rows_here, :] = conv_here
        gated = query_t[rows_here, :] * conv_here
        square_sum += jnp.sum(gated * gated, axis=0, keepdims=True)
        dot_sum += jnp.sum(grad_t[rows_here, :] * gated, axis=0, keepdims=True)
    stat_out[0:1, :] = square_sum
    stat_out[1:2, :] = dot_sum

    def send_stats(step, carry):
        peer = lax.rem(mine + step, m)
        pltpu.make_async_remote_copy(
            src_ref=stat_out,
            dst_ref=stat_in.at[mine],
            send_sem=send_sem.at[4 * len(parts)],
            recv_sem=recv_sem.at[4 * len(parts)],
            device_id=(me, peer),
            device_id_type=MESH,
        ).start()
        return carry

    lax.fori_loop(1, m, send_stats, 0)
    stat_in[mine] = stat_out[...]
    pltpu.make_async_copy(
        stat_in.at[pl.ds(0, m - 1)], stat_in.at[pl.ds(0, m - 1)], recv_sem.at[4 * len(parts)]
    ).wait()
    totals = jnp.sum(stat_in[...], axis=0)
    inverse_rms = lax.rsqrt(totals[0:1, :] / width + EPS)
    dots = totals[1:2, :] / width
    weight = inverse_rms * inverse_rms * inverse_rms * dots

    for rows_here, count, phases in pieces:
        query_here, conv_here = query_t[rows_here, :], conv_t[rows_here, :]
        dgated = inverse_rms * grad_t[rows_here, :] - weight * (query_here * conv_here)
        phases[2][1][...] = (dgated * query_here).astype(BF16).reshape(n, count, rows)
        exchange(*phases[2])
    gated = query_t[...] * conv_t[...]
    dgated = inverse_rms * grad_t[...] - weight * gated
    mixer_ref[...] = (gated * inverse_rms).T.astype(BF16)
    dquery_ref[...] = (dgated * conv_t[...]).T.astype(BF16)

    for rows_here, _, phases in pieces:
        arrived(*phases[2])
        grads = stage_first(phases[2][2][...])
        grads = jnp.concatenate([grads, grads], axis=0)
        others = jnp.concatenate([taps_spec[rows_here, :], mixed_spec[rows_here, :]], axis=0)
        grads_real, grads_imag = grads[:, :rows], grads[:, rows:]
        other_real, other_imag = others[:, :rows], others[:, rows:]
        phases[3][1][...] = stage_last(
            grads_real * other_real + grads_imag * other_imag,
            grads_imag * other_real - grads_real * other_imag,
        ).astype(BF16)
        deliver(*phases[3], 0, AHEAD)
        phases[3][2][me] = phases[3][1][me]
    for first in range(AHEAD, chips, STRIDE):
        for _, _, phases in pieces:
            deliver(*phases[3], first, min(first + STRIDE, chips))

    for rows_here, count, phases in pieces:
        arrived(*phases[3])
        dmixed = phases[3][2][:, :count, :].astype(F32).reshape(n * count, rows).T
        dkey_ref[:, rows_here] = (dmixed * value_ref[:, rows_here].astype(F32)).astype(BF16)
        dvalue_ref[:, rows_here] = (dmixed * key_ref[:, rows_here].astype(F32)).astype(BF16)
        dtaps = phases[3][2][:, count:, :].astype(F32).reshape(n * count, rows).T
        dtaps_ref[:, rows_here] = dtaps.astype(BF16)

    for _, _, phases in pieces:
        for exchanged in phases:
            sent(*exchanged)
    pltpu.make_async_copy(
        stat_in.at[pl.ds(0, m - 1)], stat_in.at[pl.ds(0, m - 1)], send_sem.at[4 * len(parts)]
    ).wait()


def store_kernel(*refs):
    sources, targets, sem = refs[:5], refs[5:10], refs[10]
    stores = [
        pltpu.make_async_copy(source, target, sem.at[number])
        for number, (source, target) in enumerate(zip(sources, targets, strict=True))
    ]
    for store in stores:
        store.start()
    for store in stores:
        store.wait()


def per_device(n, m, query, key_proj, value_proj, filter_taps, grad_out):
    rows, cols = query.shape
    group = cols // n
    length = rows * n
    consts = [jnp.asarray(table) for table in tables(n, rows)]
    where = pl.BlockSpec(memory_space=pl.ANY)
    parts = PARTS
    heights = [
        height
        for count in parts
        for height in (2 * count, 2 * count, count, count, count, count, 2 * count, 2 * count)
    ]
    wide = pltpu.VMEM((cols, rows), F32)
    local = pltpu.VMEM((rows, cols), BF16)
    shapes = [jax.ShapeDtypeStruct((rows, cols), BF16)] * 5
    results = pl.pallas_call(
        functools.partial(kernel, n, m, parts, cols * m, 1.0 / (math.sqrt(length) * length)),
        out_shape=[pltpu.VMEM((rows, cols), BF16)] * 5,
        in_specs=[where] * 11,
        out_specs=[pl.BlockSpec(memory_space=pltpu.VMEM)] * 5,
        scratch_shapes=[
            local, local, local, local, local,
            *[pltpu.VMEM(table.shape, table.dtype) for table in consts],
            [pltpu.VMEM((n, height, rows), BF16) for height in heights],
            pltpu.VMEM((8, rows), F32),
            pltpu.VMEM((m, 8, rows), F32),
            pltpu.VMEM((n * group, rows), F32),
            wide, wide, wide,
            pltpu.VMEM((n * group, 2 * rows), F32),
            pltpu.VMEM((n * group, 2 * rows), F32),
            pltpu.SemaphoreType.DMA((4 * len(parts) + 1,)),
            pltpu.SemaphoreType.DMA((4 * len(parts) + 1,)),
            pltpu.SemaphoreType.DMA((11,)),
        ],
        compiler_params=pltpu.CompilerParams(
            collective_id=0, has_side_effects=True, vmem_limit_bytes=VMEM_BYTES
        ),
    )(query, key_proj, value_proj, filter_taps, grad_out, *consts)
    return pl.pallas_call(
        store_kernel,
        out_shape=shapes,
        in_specs=[pl.BlockSpec(memory_space=pltpu.VMEM)] * 5,
        out_specs=[where] * 5,
        scratch_shapes=[pltpu.SemaphoreType.DMA((5,))],
        compiler_params=pltpu.CompilerParams(vmem_limit_bytes=8 * 1024 * 1024),
    )(*results)


def solution(mesh):
    spec = P("ctx", "tp")
    return jax.shard_map(
        functools.partial(per_device, mesh.shape["ctx"], mesh.shape["tp"]),
        mesh=mesh,
        in_specs=(spec,) * 5,
        out_specs=(spec,) * 5,
        check_vma=False,
    )
```
